32 devices in a mesh: row: 2 (over y), col: 4 (over x, core), layer: 4 (over z).
Axes of the slice: x: 2, y: 2, z: 4, core: 2. Of those that a mesh axis runs over, the one named last changes fastest.
Arguments:
- a_vals: bfloat16 [48, 4, 8, 64, 128], P('row', 'layer', 'col'), may hold values from -0.375 to 0.375
- a_cols: int32 [48, 4, 8, 2], P('row', 'layer', 'col'), may hold values from 0 to 7, as said below
- a_count: int32 [48, 4, 8], P('row', 'layer', 'col'), may hold values from 0 to 2, as said below
- panel_map: int32 [4, 8], replicated, may hold values from 0 to 7, each once within a row
- p_vals: bfloat16 [4, 8, 8, 4, 64, 256], P('layer', 'row', None, 'col'), may hold values from -6 to 6
- p_cols: int32 [4, 8, 8, 4, 4], P('layer', 'row', None, 'col'), may hold values from 0 to 7, as said below
- p_count: int32 [4, 8, 8, 4], P('layer', 'row', None, 'col'), may hold values from 0 to 4, as said below
Outputs:
- product: bfloat16 [3072, 2048], P(('row', 'col', 'layer'))
The draws below stay inside these ranges and needn't reach their ends.
Inputs may be any that keep to these rules, and one draw needn't show every extreme that they name: `a_count`: each block row has at most 27 valid operator blocks in all, some block row exactly 27, and some entry reaches 2. `a_cols`: the slots of one block row and section name distinct block columns. `p_cols`: the slots of one block row and group name distinct coarse columns. `p_count`: reaches 4 somewhere in every draw.
All inputs are finite; a program needn't handle non-finite values.
Results may differ from the reference program's by a relative error of at most 0.001.
Values may be sent and summed in bfloat16 or wider, within the bound.
A program may use at most 128 MiB of HBM per device.

```python
import jax
import jax.numpy as jnp
from jax import lax

B = 64
NST = 8
SA = 2
SP = 4
CB = 8
PW = 8
NBR = 48
N_COL = 4
N_LAYER = 4


def draw_a_count(key, part):
    slot_total = N_LAYER * NST * SA
    section_total = N_LAYER * NST
    keys = jax.random.split(jax.random.fold_in(key, 11), NBR)
    orders = jax.vmap(lambda single: jax.random.permutation(single, slot_total))(keys)
    heavy = jax.random.randint(jax.random.fold_in(key, 12), (NBR,), 0, 4) == 0
    position = jax.random.randint(jax.random.fold_in(key, 13), (), 0, NBR)
    forced = jnp.arange(NBR, dtype=jnp.int32) == position
    orders = jnp.where(forced[:, None], jnp.arange(slot_total, dtype=jnp.int32)[None, :], orders)
    light = jax.random.randint(jax.random.fold_in(key, 14), (NBR,), 12, 28)
    taken_count = jnp.where(heavy | forced, 27, light)
    taken = jnp.arange(slot_total, dtype=jnp.int32)[None, :] < taken_count[:, None]
    section_of = orders // SA
    hits = (section_of[:, :, None] == jnp.arange(section_total, dtype=jnp.int32)[None, None, :]) & taken[:, :, None]
    counts = jnp.sum(hits.astype(jnp.int32), axis=1)
    return counts.reshape(NBR, N_LAYER, NST).astype(jnp.int32)


def draw_a_cols(key, part):
    total = NBR * N_LAYER * NST
    keys = jax.random.split(jax.random.fold_in(key, 41), total)
    chosen = jax.vmap(lambda single: jax.random.permutation(single, PW)[:SA])(keys)
    return chosen.reshape(NBR, N_LAYER, NST, SA).astype(jnp.int32)


def draw_p_cols(key, part):
    total = N_LAYER * NST * PW * N_COL
    keys = jax.random.split(jax.random.fold_in(key, 21), total)
    chosen = jax.vmap(lambda single: jax.random.permutation(single, CB)[:SP])(keys)
    return chosen.reshape(N_LAYER, NST, PW, N_COL, SP).astype(jnp.int32)


def draw_p_count(key, part):
    total = N_LAYER * NST * PW * N_COL
    base_count = jax.random.randint(jax.random.fold_in(key, 31), (total,), 0, SP // 2 + 1)
    position = jax.random.randint(jax.random.fold_in(key, 32), (), 0, total)
    filled = jnp.where(jnp.arange(total, dtype=jnp.int32) == position, SP, base_count)
    return filled.reshape(N_LAYER, NST, PW, N_COL).astype(jnp.int32)


def steps_of(key, shape, cuts, low, top_value):
    def one(dim, parts):
        heights = jax.random.uniform(jax.random.fold_in(jax.random.fold_in(key, 6), dim), (parts,), jnp.float32, low / len(cuts), top_value / len(cuts))
        return jnp.repeat(jnp.exp(heights), shape[dim] // parts).reshape((-1,) + (1,) * (len(shape) - dim - 1))

    loudness = one(*cuts[0])
    for cut in cuts[1:]:
        loudness = loudness * one(*cut)
    return loudness


def gaussian(key, dims, width, most, pieces=(), kind=jnp.bfloat16):
    gain = steps_of(key, dims, pieces, -0.22, 0.18) if pieces else 1.0
    drawn = jax.random.normal(key, dims, jnp.float32) * width * gain
    return jnp.minimum(jnp.maximum(drawn, -most), most).astype(kind)


def setup_inputs(seed: int = 0) -> dict:
    key_of = jax.random.split(jax.random.key(seed), 8)
    return {
        "a_vals": gaussian(key_of[0], (NBR, N_LAYER, NST, B, SA * B), (4 * B) ** -0.5, 0.375, ((0, 2), (1, 4), (2, 4))),
        "a_cols": draw_a_cols(jax.random.fold_in(key_of[7], 71), 0),
        "a_count": draw_a_count(jax.random.fold_in(key_of[7], 71), 0),
        "panel_map": jax.vmap(lambda own: jax.random.permutation(own, NST))(jax.random.split(key_of[3], N_LAYER)).reshape((N_LAYER, NST)).astype(jnp.int32),
        "p_vals": gaussian(key_of[4], (N_LAYER, NST, PW, N_COL, B, SP * B), 1.0, 6.0, ((0, 4), (1, 2), (3, 4))),
        "p_cols": draw_p_cols(jax.random.fold_in(key_of[7], 71), 0),
        "p_count": draw_p_count(jax.random.fold_in(key_of[7], 71), 0),
    }


def reference(a_vals, a_cols, a_count, panel_map, p_vals, p_cols, p_count):
    block_side = a_vals.shape[3]
    slot_a = a_cols.shape[3]
    slot_p = p_cols.shape[4]
    layers = panel_map.shape[0]
    sections = panel_map.shape[1]
    p_width = p_vals.shape[2]
    groups = p_vals.shape[3]
    flat_rows = layers * sections * p_width
    p_flat = p_vals.reshape(flat_rows, groups, block_side, slot_p, block_side)
    pcol_flat = p_cols.reshape(flat_rows, groups, slot_p)
    pcount_flat = p_count.reshape(flat_rows, groups)
    panel_base = (jnp.arange(layers, dtype=jnp.int32)[:, None] * sections + panel_map.astype(jnp.int32)) * p_width

    def one_row(inputs):
        row_vals, row_cols, row_count = inputs
        a_blocks = row_vals.astype(jnp.float32).reshape(layers, sections, block_side, slot_a, block_side)
        a_mask = (jnp.arange(slot_a, dtype=jnp.int32)[None, None, :] < row_count[:, :, None]).astype(jnp.float32)
        a_blocks = a_blocks * a_mask[:, :, None, :, None]
        k_index = (panel_base[:, :, None] + row_cols).astype(jnp.int32)
        p_blocks = p_flat[k_index].astype(jnp.float32)
        p_mask = (jnp.arange(slot_p, dtype=jnp.int32) < pcount_flat[k_index][..., None]).astype(jnp.float32)
        onehot = (pcol_flat[k_index][..., None] == jnp.arange(CB, dtype=jnp.int32)).astype(jnp.float32) * p_mask[..., None]
        products = jnp.einsum("lsxay,lsagytz->lsagtxz", a_blocks, p_blocks, precision=lax.Precision.HIGHEST)
        row_out = jnp.einsum("lsagtxz,lsagtc->xgcz", products, onehot, precision=lax.Precision.HIGHEST)
        return row_out.reshape(block_side, groups * CB * block_side)

    stacked = lax.map(one_row, (a_vals, a_cols, a_count))
    return stacked.reshape(-1, groups * CB * block_side).astype(jnp.bfloat16)
```

```python
import functools

import jax
import jax.numpy as jnp
from jax import lax
from jax.experimental import pallas as pl
from jax.experimental.pallas import tpu as pltpu
from jax.sharding import PartitionSpec as P

CB = 8
MESH = pl.DeviceIdType.MESH


def swap_halves(tile):
    return pltpu.roll(tile.astype(jnp.float32), 64, 1).astype(jnp.bfloat16)


def masks_of(meta_row, lane_high):
    straight = (meta_row - lane_high).astype(jnp.float32)
    swapped = pltpu.roll(meta_row, 64, 1) - lane_high
    wide = lambda row: jnp.broadcast_to(row, (16, 128)).astype(jnp.bfloat16)
    return wide(straight), wide(swapped)


def kernel(
    sizes,
    pm_ref, a_ref, am_ref, p_ref, pq_ref, out_ref,
    ag, amg, pg, pqg, dense, lhs, part, up_in, down_in, fin, got,
    p_s, p_r, q_s, q_r, a_s, a_r, m_s, m_r, u_s, u_r, d_s, d_r, o_s, o_r,
):
    R, C, L = sizes
    row, col, layer = lax.axis_index("row"), lax.axis_index("col"), lax.axis_index("layer")
    panels_held, width_p = p_ref.shape[0], p_ref.shape[1]
    blocks, held = a_ref.shape[1], a_ref.shape[2]
    mate = col + 1 - 2 * lax.rem(col, 2)
    across = lax.rem(col + 2, 4)
    far = lax.rem(mate + 2, 4)
    owners = (col, mate, across, far)

    barrier = pltpu.get_barrier_semaphore()
    for j in range(1, R):
        pl.semaphore_signal(barrier, inc=1, device_id={"row": lax.rem(row + j, R)}, device_id_type=MESH)
    for j in range(1, C):
        pl.semaphore_signal(barrier, inc=1, device_id={"col": lax.rem(col + j, C)}, device_id_type=MESH)

    @pl.when(layer > 0)
    def _():
        pl.semaphore_signal(barrier, inc=1, device_id={"layer": layer - 1}, device_id_type=MESH)

    @pl.when(layer < L - 1)
    def _():
        pl.semaphore_signal(barrier, inc=1, device_id={"layer": layer + 1}, device_id_type=MESH)

    ends = (layer > 0).astype(jnp.int32) + (layer < L - 1).astype(jnp.int32)
    pl.semaphore_wait(barrier, R - 1 + C - 1 + ends)

    def remote(src, dst, send, recv, device):
        return pltpu.make_async_remote_copy(
            src_ref=src, dst_ref=dst, send_sem=send, recv_sem=recv, device_id=device, device_id_type=MESH
        )

    def p_copy(j, i, slot):
        return remote(p_ref.at[i], pg.at[slot, i], p_s.at[j, i], p_r.at[j, i], {"row": lax.rem(row + j, R)})

    def q_copy(j, slot):
        return remote(pq_ref, pqg.at[slot], q_s.at[j], q_r.at[j], {"row": lax.rem(row + j, R)})

    def a_copy(x, c):
        src = ag.at[1, c] if x == 3 else a_ref.at[c]
        return remote(src, ag.at[x - 1, c], a_s.at[x, c], a_r.at[x, c], {"col": across if x == 2 else mate})

    def m_copy(x):
        src = amg.at[1] if x == 3 else am_ref
        return remote(src, amg.at[x - 1], m_s.at[x], m_r.at[x], {"col": across if x == 2 else mate})

    for j in range(1, R):
        q_copy(j, row).start()
    m_copy(2).start()
    m_copy(1).start()
    for i in range(panels_held):
        for j in range(1, R):
            p_copy(j, i, row).start()
    for c in range(C):
        a_copy(2, c).start()
    for c in range(C):
        a_copy(1, c).start()

    lane_high = (lax.broadcasted_iota(jnp.int32, (1, 128), 1) >= 64).astype(jnp.float32)
    zero = jnp.zeros((4, 16, 128), jnp.bfloat16)

    def spread(tiles, keys, m):
        value = zero
        for tile, key in zip(tiles, keys):
            value = jnp.where((key == jnp.bfloat16(2 * m))[None], tile, value)
        return value.reshape(64, 128)

    def expand_panel(vals, meta, i, q):
        for w in range(width_p):
            tiles, keys = [], []
            for half in range(2):
                tile = vals[i, w, :, half * 128 : half * 128 + 128]
                tiles += [tile.reshape(4, 16, 128), swap_halves(tile).reshape(4, 16, 128)]
                keys += masks_of(meta[i, 2 * w + half : 2 * w + half + 1, :], lane_high)
            for m in range(CB // 2):
                dense[q, w * 64 : w * 64 + 64, m * 128 : m * 128 + 128] = spread(tiles, keys, m)

    @pl.loop(0, panels_held)
    def _(i):
        expand_panel(p_ref, pq_ref, i, row * panels_held + i)

    m_copy(2).wait_recv()
    m_copy(3).start()
    for c in range(C):
        a_copy(2, c).wait_recv()
        a_copy(3, c).start()

    for j in range(1, R):
        slot = lax.rem(row + R - j, R)
        q_copy(j, slot).wait_recv()

        @pl.loop(0, panels_held)
        def _(i):
            p_copy(j, i, slot).wait_recv()
            expand_panel(pg.at[slot], pqg.at[slot], i, slot * panels_held + i)

    m_copy(1).wait_recv()
    m_copy(3).wait_recv()

    def u_copy(d, c):
        return remote(part.at[c, d], up_in.at[c, d], u_s.at[c, d], u_r.at[c, d], {"layer": layer + 1})

    def d_copy(d, c):
        return remote(part.at[c, d], down_in.at[c, d], d_s.at[c, d], d_r.at[c, d], {"layer": layer - 1})

    rows_c = blocks * 64

    @pl.loop(0, C)
    def _(c):
        a_copy(1, c).wait_recv()
        a_copy(3, c).wait_recv()
        total = None
        for x in range(4):
            vals = a_ref if x == 0 else ag.at[x - 1]
            meta = am_ref if x == 0 else amg.at[x - 1]
            for k in range(held):
                slot = (x * held + k) % 2
                for b in range(blocks):
                    tile = vals[c, b, k]
                    tiles = [tile.reshape(4, 16, 128), swap_halves(tile).reshape(4, 16, 128)]
                    line = b * held + k
                    keys = masks_of(meta[c, line : line + 1, :], lane_high)
                    for m in range(CB // 2):
                        lhs[slot, b * 64 : b * 64 + 64, m * 128 : m * 128 + 128] = spread(tiles, keys, m)
                panel = pm_ref[layer, owners[x] * held + k]
                term = jnp.dot(lhs[slot], dense[panel], preferred_element_type=jnp.float32)
                total = term if total is None else total + term
        part[c] = total.reshape(part.shape[1:])

        @pl.when(layer == 0)
        def _():
            for d in range(L - 1, 0, -1):
                u_copy(d, c).start()

        @pl.when(layer == L - 1)
        def _():
            for d in range(L - 1):
                d_copy(d, c).start()

    def forward_up(c, d):
        @pl.when((layer > 0) & (layer < d))
        def _():
            u_copy(d, c).wait_recv()
            part[c, d] += up_in[c, d]
            u_copy(d, c).start()

    def forward_down(c, d):
        @pl.when((layer < L - 1) & (layer > d))
        def _():
            d_copy(d, c).wait_recv()
            part[c, d] += down_in[c, d]
            d_copy(d, c).start()

    def o_copy(c, slot):
        return remote(fin.at[c], got.at[slot], o_s.at[c], o_r.at[slot], {"col": c})

    @pl.loop(0, C)
    def _(c):
        for k in range(L - 1):
            @pl.when(layer >= L // 2)
            def _():
                forward_down(c, k)

            forward_up(c, L - 1 - k)

            @pl.when(layer < L // 2)
            def _():
                forward_down(c, k)

        @pl.when(layer > 0)
        def _():
            u_copy(layer, c).wait_recv()
            part[c, layer] += up_in[c, layer]

        @pl.when(layer < L - 1)
        def _():
            d_copy(layer, c).wait_recv()
            part[c, layer] += down_in[c, layer]

        result = part[c, layer].astype(jnp.bfloat16)

        @pl.when(col == c)
        def _():
            got[c] = result

        @pl.when(col != c)
        def _():
            fin[c] = result
            o_copy(c, col).start()

    for c in range(C):
        @pl.when(col != c)
        def _():
            o_copy(c, c).wait_recv()

        out_ref[:, c * CB * 64 : (c + 1) * CB * 64] = got[c]

    for j in range(1, R):
        q_copy(j, row).wait_send()
        for i in range(panels_held):
            p_copy(j, i, row).wait_send()
    for x in range(1, 4):
        m_copy(x).wait_send()
        for c in range(C):
            a_copy(x, c).wait_send()
    for c in range(C):
        for d in range(L):
            @pl.when(layer < d)
            def _():
                u_copy(d, c).wait_send()

            @pl.when(layer > d)
            def _():
                d_copy(d, c).wait_send()

        @pl.when(col != c)
        def _():
            o_copy(c, c).wait_send()


def lanes_of(cols, count):
    slots = cols.shape[-1]
    valid = jnp.arange(slots) < count[..., None]
    key = jnp.where(valid, cols, -64).astype(jnp.float32)
    wide = jnp.broadcast_to(key[..., None], key.shape + (64,))
    return wide.reshape(cols.shape[:-1] + (slots // 2, 128))


def body(sizes, a_vals, a_cols, a_count, panel_map, p_vals, p_cols, p_count):
    R, C, L = sizes
    rows_blk, _, held, side, wide = a_vals.shape
    blocks = rows_blk // C
    panels_held, width_p = p_vals.shape[1], p_vals.shape[2]
    a = a_vals.reshape(C, blocks, held, side, wide)
    lines = blocks * held
    am = lanes_of(a_cols[:, 0], a_count[:, 0]).reshape(C, lines, 128)
    pad = -lines % 8
    am = jnp.pad(am, ((0, 0), (0, pad), (0, 0)))
    p = p_vals.reshape(panels_held, width_p, side, p_vals.shape[-1])
    pq = lanes_of(p_cols[0, :, :, 0], p_count[0, :, :, 0]).reshape(panels_held, 2 * width_p, 128)
    piece = blocks * side // L
    width = CB * side
    f32, bf16 = jnp.float32, jnp.bfloat16
    sems = pltpu.SemaphoreType.DMA
    vmem = pl.BlockSpec(memory_space=pltpu.VMEM)
    return pl.pallas_call(
        functools.partial(kernel, sizes),
        out_shape=jax.ShapeDtypeStruct((piece, C * width), bf16),
        in_specs=[pl.BlockSpec(memory_space=pltpu.SMEM), vmem, vmem, vmem, vmem],
        out_specs=vmem,
        scratch_shapes=[
            pltpu.VMEM((3,) + a.shape, bf16),
            pltpu.VMEM((3,) + am.shape, f32),
            pltpu.VMEM((R,) + p.shape, bf16),
            pltpu.VMEM((R,) + pq.shape, f32),
            pltpu.VMEM((R * panels_held, width_p * side, width), bf16),
            pltpu.VMEM((2, blocks * side, width_p * side), bf16),
            pltpu.VMEM((C, L, piece, width), f32),
            pltpu.VMEM((C, L, piece, width), f32),
            pltpu.VMEM((C, L, piece, width), f32),
            pltpu.VMEM((C, piece, width), bf16),
            pltpu.VMEM((C, piece, width), bf16),
            sems((R, panels_held)), sems((R, panels_held)), sems((R,)), sems((R,)),
            sems((4, C)), sems((4, C)), sems((4,)), sems((4,)),
            sems((C, L)), sems((C, L)), sems((C, L)), sems((C, L)),
            sems((C,)), sems((C,)),
        ],
        compiler_params=pltpu.CompilerParams(
            collective_id=0, has_side_effects=True, vmem_limit_bytes=56 * 1024 * 1024
        ),
        cost_estimate=pl.CostEstimate(flops=7 * 10**9, bytes_accessed=3 * 10**6, transcendentals=0),
    )(panel_map, a, am, p, pq)


def solution(mesh):
    placed = (
        P("row", "layer", "col", None, None),
        P("row", "layer", "col", None),
        P("row", "layer", "col"),
        P(),
        P("layer", "row", None, "col", None, None),
        P("layer", "row", None, "col", None),
        P("layer", "row", None, "col"),
    )
    sizes = (mesh.shape["row"], mesh.shape["col"], mesh.shape["layer"])
    return jax.shard_map(
        functools.partial(body, sizes),
        mesh=mesh,
        in_specs=placed,
        out_specs=P(("row", "col", "layer"), None),
        check_vma=False,
    )
```

```python
import functools

import jax
import jax.numpy as jnp
from jax import lax
from jax.experimental import pallas as pl
from jax.experimental.pallas import tpu as pltpu
from jax.sharding import PartitionSpec as P

CB = 8
MESH = pl.DeviceIdType.MESH


def swap_halves(tile):
    return pltpu.roll(tile.astype(jnp.float32), 64, 1).astype(jnp.bfloat16)


def masks_of(meta_row, lane_high):
    straight = (meta_row - lane_high).astype(jnp.float32)
    swapped = pltpu.roll(meta_row, 64, 1) - lane_high
    wide = lambda row: jnp.broadcast_to(row, (16, 128)).astype(jnp.bfloat16)
    return wide(straight), wide(swapped)


FULL = float(2**22)


def encode(value):
    rows, width = value.shape
    grouped = value.reshape(rows // 8, 8, width)
    most = jnp.max(jnp.abs(grouped), axis=0)
    most = functools.reduce(jnp.maximum, [most[:, i : i + 128] for i in range(0, width, 128)])
    most = jnp.maximum(most, 1e-31)
    factor = jnp.concatenate([FULL / most] * (width // 128), axis=1)
    fixed = jnp.round(grouped * factor[None]).astype(jnp.int32).reshape(rows, width)
    high = lax.shift_right_arithmetic(fixed, 8).astype(jnp.int16)
    low = fixed & 255
    low = (low[:, : width // 2] * 256 + low[:, width // 2 :] - 32768).astype(jnp.int16)
    return high, low, most * (1.0 / FULL)


def decode(high, low, scale):
    rows, width = high.shape
    pair = low.astype(jnp.int32) + 32768
    low = jnp.concatenate([lax.shift_right_arithmetic(pair, 8), pair & 255], axis=1)
    fixed = (high.astype(jnp.int32) * 256 + low).astype(jnp.float32)
    factor = jnp.concatenate([scale] * (width // 128), axis=1)
    return (fixed.reshape(rows // 8, 8, width) * factor[None]).reshape(rows, width)


def kernel(
    sizes,
    pm_ref, a_ref, am_ref, p_ref, pq_ref, out_ref,
    ag, amg, pg, pqg, dense, lhs, part, tx, txs, up_in, up_sc, down_in, down_sc, fin, got,
    p_s, p_r, q_s, q_r, a_s, a_r, m_s, m_r, u_s, u_r, us_s, us_r, d_s, d_r, ds_s, ds_r, o_s, o_r,
):
    R, C, L = sizes
    row, col, layer = lax.axis_index("row"), lax.axis_index("col"), lax.axis_index("layer")
    panels_held, width_p = p_ref.shape[0], p_ref.shape[1]
    blocks, held = a_ref.shape[1], a_ref.shape[2]
    mate = col + 1 - 2 * lax.rem(col, 2)
    across = lax.rem(col + 2, 4)
    far = lax.rem(mate + 2, 4)
    owners = (col, mate, across, far)

    barrier = pltpu.get_barrier_semaphore()
    for j in range(1, R):
        pl.semaphore_signal(barrier, inc=1, device_id={"row": lax.rem(row + j, R)}, device_id_type=MESH)
    for j in range(1, C):
        pl.semaphore_signal(barrier, inc=1, device_id={"col": lax.rem(col + j, C)}, device_id_type=MESH)

    @pl.when(layer > 0)
    def _():
        pl.semaphore_signal(barrier, inc=1, device_id={"layer": layer - 1}, device_id_type=MESH)

    @pl.when(layer < L - 1)
    def _():
        pl.semaphore_signal(barrier, inc=1, device_id={"layer": layer + 1}, device_id_type=MESH)

    ends = (layer > 0).astype(jnp.int32) + (layer < L - 1).astype(jnp.int32)
    pl.semaphore_wait(barrier, R - 1 + C - 1 + ends)

    def remote(src, dst, send, recv, device):
        return pltpu.make_async_remote_copy(
            src_ref=src, dst_ref=dst, send_sem=send, recv_sem=recv, device_id=device, device_id_type=MESH
        )

    def p_copy(j, i, slot):
        return remote(p_ref.at[i], pg.at[slot, i], p_s.at[j, i], p_r.at[j, i], {"row": lax.rem(row + j, R)})

    def q_copy(j, slot):
        return remote(pq_ref, pqg.at[slot], q_s.at[j], q_r.at[j], {"row": lax.rem(row + j, R)})

    def a_copy(x, c):
        src = ag.at[1, c] if x == 3 else a_ref.at[c]
        return remote(src, ag.at[x - 1, c], a_s.at[x, c], a_r.at[x, c], {"col": across if x == 2 else mate})

    def m_copy(x):
        src = amg.at[1] if x == 3 else am_ref
        return remote(src, amg.at[x - 1], m_s.at[x], m_r.at[x], {"col": across if x == 2 else mate})

    for j in range(1, R):
        q_copy(j, row).start()
    m_copy(2).start()
    m_copy(1).start()
    for i in range(panels_held):
        for j in range(1, R):
            p_copy(j, i, row).start()
    for c in range(C):
        a_copy(2, c).start()
    for c in range(C):
        a_copy(1, c).start()

    lane_high = (lax.broadcasted_iota(jnp.int32, (1, 128), 1) >= 64).astype(jnp.float32)
    zero = jnp.zeros((4, 16, 128), jnp.bfloat16)

    def spread(tiles, keys, m):
        value = zero
        for tile, key in zip(tiles, keys):
            value = jnp.where((key == jnp.bfloat16(2 * m))[None], tile, value)
        return value.reshape(64, 128)

    def expand_panel(vals, meta, i, q):
        for w in range(width_p):
            tiles, keys = [], []
            for half in range(2):
                tile = vals[i, w, :, half * 128 : half * 128 + 128]
                tiles += [tile.reshape(4, 16, 128), swap_halves(tile).reshape(4, 16, 128)]
                keys += masks_of(meta[i, 2 * w + half : 2 * w + half + 1, :], lane_high)
            for m in range(CB // 2):
                dense[q, w * 64 : w * 64 + 64, m * 128 : m * 128 + 128] = spread(tiles, keys, m)

    @pl.loop(0, panels_held)
    def _(i):
        expand_panel(p_ref, pq_ref, i, row * panels_held + i)

    m_copy(2).wait_recv()
    m_copy(3).start()
    for c in range(C):
        a_copy(2, c).wait_recv()
        a_copy(3, c).start()

    for j in range(1, R):
        slot = lax.rem(row + R - j, R)
        q_copy(j, slot).wait_recv()

        @pl.loop(0, panels_held)
        def _(i):
            p_copy(j, i, slot).wait_recv()
            expand_panel(pg.at[slot], pqg.at[slot], i, slot * panels_held + i)

    m_copy(1).wait_recv()
    m_copy(3).wait_recv()

    wide_out = part.shape[3]

    def u_copies(d, c):
        to = {"layer": layer + 1}
        return (
            remote(txs.at[c, d], up_sc.at[c, d], us_s.at[c, d], us_r.at[c, d], to),
            remote(tx.at[c, d], up_in.at[c, d], u_s.at[c, d], u_r.at[c, d], to),
        )

    def d_copies(d, c):
        to = {"layer": layer - 1}
        return (
            remote(txs.at[c, d], down_sc.at[c, d], ds_s.at[c, d], ds_r.at[c, d], to),
            remote(tx.at[c, d], down_in.at[c, d], d_s.at[c, d], d_r.at[c, d], to),
        )

    def send(copies, d, c, value):
        high, low, scale = encode(value)
        tx[c, d, :, :wide_out] = high
        tx[c, d, :, wide_out:] = low
        txs[c, d] = scale
        for copy in copies(d, c):
            copy.start()

    def received(copies, ref, scales, d, c):
        for copy in copies(d, c):
            copy.wait_recv()
        return decode(ref[c, d, :, :wide_out], ref[c, d, :, wide_out:], scales[c, d])

    @pl.loop(0, C)
    def _(c):
        a_copy(1, c).wait_recv()
        a_copy(3, c).wait_recv()
        total = None
        for x in range(4):
            vals = a_ref if x == 0 else ag.at[x - 1]
            meta = am_ref if x == 0 else amg.at[x - 1]
            for k in range(held):
                slot = (x * held + k) % 2
                for b in range(blocks):
                    tile = vals[c, b, k]
                    tiles = [tile.reshape(4, 16, 128), swap_halves(tile).reshape(4, 16, 128)]
                    line = b * held + k
                    keys = masks_of(meta[c, line : line + 1, :], lane_high)
                    for m in range(CB // 2):
                        lhs[slot, b * 64 : b * 64 + 64, m * 128 : m * 128 + 128] = spread(tiles, keys, m)
                panel = pm_ref[layer, owners[x] * held + k]
                term = jnp.dot(lhs[slot], dense[panel], preferred_element_type=jnp.float32)
                total = term if total is None else total + term
        part[c] = total.reshape(part.shape[1:])

        @pl.when(layer == 0)
        def _():
            for d in range(L - 1, 0, -1):
                send(u_copies, d, c, part[c, d])

        @pl.when(layer == L - 1)
        def _():
            for d in range(L - 1):
                send(d_copies, d, c, part[c, d])

    def forward_up(c, d):
        @pl.when((layer > 0) & (layer < d))
        def _():
            send(u_copies, d, c, part[c, d] + received(u_copies, up_in, up_sc, d, c))

    def forward_down(c, d):
        @pl.when((layer < L - 1) & (layer > d))
        def _():
            send(d_copies, d, c, part[c, d] + received(d_copies, down_in, down_sc, d, c))

    def o_copy(c, slot):
        return remote(fin.at[c], got.at[slot], o_s.at[c], o_r.at[slot], {"col": c})

    @pl.loop(0, C)
    def _(c):
        for k in range(L - 1):
            @pl.when(layer >= L // 2)
            def _():
                forward_down(c, k)

            forward_up(c, L - 1 - k)

            @pl.when(layer < L // 2)
            def _():
                forward_down(c, k)

        @pl.when(layer > 0)
        def _():
            part[c, layer] += received(u_copies, up_in, up_sc, layer, c)

        @pl.when(layer < L - 1)
        def _():
            part[c, layer] += received(d_copies, down_in, down_sc, layer, c)

        result = part[c, layer].astype(jnp.bfloat16)

        @pl.when(col == c)
        def _():
            got[c] = result

        @pl.when(col != c)
        def _():
            fin[c] = result
            o_copy(c, col).start()

    for c in range(C):
        @pl.when(col != c)
        def _():
            o_copy(c, c).wait_recv()

        out_ref[:, c * CB * 64 : (c + 1) * CB * 64] = got[c]

    for j in range(1, R):
        q_copy(j, row).wait_send()
        for i in range(panels_held):
            p_copy(j, i, row).wait_send()
    for x in range(1, 4):
        m_copy(x).wait_send()
        for c in range(C):
            a_copy(x, c).wait_send()
    for c in range(C):
        for d in range(L):
            @pl.when(layer < d)
            def _():
                for copy in u_copies(d, c):
                    copy.wait_send()

            @pl.when(layer > d)
            def _():
                for copy in d_copies(d, c):
                    copy.wait_send()

        @pl.when(col != c)
        def _():
            o_copy(c, c).wait_send()


def lanes_of(cols, count):
    slots = cols.shape[-1]
    valid = jnp.arange(slots) < count[..., None]
    key = jnp.where(valid, cols, -64).astype(jnp.float32)
    wide = jnp.broadcast_to(key[..., None], key.shape + (64,))
    return wide.reshape(cols.shape[:-1] + (slots // 2, 128))


def body(sizes, a_vals, a_cols, a_count, panel_map, p_vals, p_cols, p_count):
    R, C, L = sizes
    rows_blk, _, held, side, wide = a_vals.shape
    blocks = rows_blk // C
    panels_held, width_p = p_vals.shape[1], p_vals.shape[2]
    a = a_vals.reshape(C, blocks, held, side, wide)
    lines = blocks * held
    am = lanes_of(a_cols[:, 0], a_count[:, 0]).reshape(C, lines, 128)
    pad = -lines % 8
    am = jnp.pad(am, ((0, 0), (0, pad), (0, 0)))
    p = p_vals.reshape(panels_held, width_p, side, p_vals.shape[-1])
    pq = lanes_of(p_cols[0, :, :, 0], p_count[0, :, :, 0]).reshape(panels_held, 2 * width_p, 128)
    piece = blocks * side // L
    width = CB * side
    f32, bf16 = jnp.float32, jnp.bfloat16
    sems = pltpu.SemaphoreType.DMA
    coded = pltpu.VMEM((C, L, piece, width + width // 2), jnp.int16)
    scales = pltpu.VMEM((C, L, 8, 128), f32)
    vmem = pl.BlockSpec(memory_space=pltpu.VMEM)
    return pl.pallas_call(
        functools.partial(kernel, sizes),
        out_shape=jax.ShapeDtypeStruct((piece, C * width), bf16),
        in_specs=[pl.BlockSpec(memory_space=pltpu.SMEM), vmem, vmem, vmem, vmem],
        out_specs=vmem,
        scratch_shapes=[
            pltpu.VMEM((3,) + a.shape, bf16),
            pltpu.VMEM((3,) + am.shape, f32),
            pltpu.VMEM((R,) + p.shape, bf16),
            pltpu.VMEM((R,) + pq.shape, f32),
            pltpu.VMEM((R * panels_held, width_p * side, width), bf16),
            pltpu.VMEM((2, blocks * side, width_p * side), bf16),
            pltpu.VMEM((C, L, piece, width), f32),
            *[coded, scales] * 3,
            pltpu.VMEM((C, piece, width), bf16),
            pltpu.VMEM((C, piece, width), bf16),
            sems((R, panels_held)), sems((R, panels_held)), sems((R,)), sems((R,)),
            sems((4, C)), sems((4, C)), sems((4,)), sems((4,)),
            *[sems((C, L))] * 8,
            sems((C,)), sems((C,)),
        ],
        compiler_params=pltpu.CompilerParams(
            collective_id=0, has_side_effects=True, vmem_limit_bytes=56 * 1024 * 1024
        ),
        cost_estimate=pl.CostEstimate(flops=7 * 10**9, bytes_accessed=3 * 10**6, transcendentals=0),
    )(panel_map, a, am, p, pq)


def solution(mesh):
    placed = (
        P("row", "layer", "col", None, None),
        P("row", "layer", "col", None),
        P("row", "layer", "col"),
        P(),
        P("layer", "row", None, "col", None, None),
        P("layer", "row", None, "col", None),
        P("layer", "row", None, "col"),
    )
    sizes = (mesh.shape["row"], mesh.shape["col"], mesh.shape["layer"])
    return jax.shard_map(
        functools.partial(body, sizes),
        mesh=mesh,
        in_specs=placed,
        out_specs=P(("row", "col", "layer"), None),
        check_vma=False,
    )
```

```python
import functools

import jax
import jax.numpy as jnp
from jax import lax
from jax.experimental import pallas as pl
from jax.experimental.pallas import tpu as pltpu
from jax.sharding import PartitionSpec as P

CB = 8
MESH = pl.DeviceIdType.MESH


def swap_halves(tile):
    return pltpu.roll(tile.astype(jnp.float32), 64, 1).astype(jnp.bfloat16)


def masks_of(meta_row, lane_high):
    straight = (meta_row - lane_high).astype(jnp.float32)
    swapped = pltpu.roll(meta_row, 64, 1) - lane_high
    wide = lambda row: jnp.broadcast_to(row, (16, 128)).astype(jnp.bfloat16)
    return wide(straight), wide(swapped)


FULL = float(2**22)


def encode(value):
    rows, width = value.shape
    grouped = value.reshape(rows // 8, 8, width)
    most = jnp.max(jnp.abs(grouped), axis=0)
    most = functools.reduce(jnp.maximum, [most[:, i : i + 128] for i in range(0, width, 128)])
    most = jnp.maximum(most, 1e-31)
    factor = jnp.concatenate([FULL / most] * (width // 128), axis=1)
    fixed = jnp.round(grouped * factor[None]).astype(jnp.int32).reshape(rows, width)
    high = lax.shift_right_arithmetic(fixed, 8).astype(jnp.int16)
    low = fixed & 255
    low = (low[:, : width // 2] * 256 + low[:, width // 2 :] - 32768).astype(jnp.int16)
    return high, low, most * (1.0 / FULL)


def decode(high, low, scale):
    rows, width = high.shape
    pair = low.astype(jnp.int32) + 32768
    low = jnp.concatenate([lax.shift_right_arithmetic(pair, 8), pair & 255], axis=1)
    fixed = (high.astype(jnp.int32) * 256 + low).astype(jnp.float32)
    factor = jnp.concatenate([scale] * (width // 128), axis=1)
    return (fixed.reshape(rows // 8, 8, width) * factor[None]).reshape(rows, width)


def kernel(
    sizes,
    slot_ref, a_ref, am_ref, p_ref, pq_ref, out_ref,
    ag, amg, pg, pqg, dense, lhs, part, tx, txs, up_in, up_sc, down_in, down_sc, fin, got,
    p_s, p_r, q_s, q_r, a_s, a_r, m_s, m_r, u_s, u_r, us_s, us_r, d_s, d_r, ds_s, ds_r, o_s, o_r,
):
    R, C, L = sizes
    row, col, layer = lax.axis_index("row"), lax.axis_index("col"), lax.axis_index("layer")
    panels_held, width_p = p_ref.shape[0], p_ref.shape[1]
    blocks, held = a_ref.shape[1], a_ref.shape[2]
    mate = col + 1 - 2 * lax.rem(col, 2)
    across = lax.rem(col + 2, 4)

    barrier = pltpu.get_barrier_semaphore()
    for j in range(1, R):
        pl.semaphore_signal(barrier, inc=1, device_id={"row": lax.rem(row + j, R)}, device_id_type=MESH)
    for j in range(1, C):
        pl.semaphore_signal(barrier, inc=1, device_id={"col": lax.rem(col + j, C)}, device_id_type=MESH)

    @pl.when(layer > 0)
    def _():
        pl.semaphore_signal(barrier, inc=1, device_id={"layer": layer - 1}, device_id_type=MESH)

    @pl.when(layer < L - 1)
    def _():
        pl.semaphore_signal(barrier, inc=1, device_id={"layer": layer + 1}, device_id_type=MESH)

    ends = (layer > 0).astype(jnp.int32) + (layer < L - 1).astype(jnp.int32)
    pl.semaphore_wait(barrier, R - 1 + C - 1 + ends)

    def remote(src, dst, send, recv, device):
        return pltpu.make_async_remote_copy(
            src_ref=src, dst_ref=dst, send_sem=send, recv_sem=recv, device_id=device, device_id_type=MESH
        )

    def p_copy(j, i, slot):
        return remote(p_ref.at[i], pg.at[slot, i], p_s.at[j, i], p_r.at[j, i], {"row": lax.rem(row + j, R)})

    def q_copy(j, slot):
        return remote(pq_ref, pqg.at[slot], q_s.at[j], q_r.at[j], {"row": lax.rem(row + j, R)})

    def a_copy(x, c):
        src = ag.at[1, c] if x == 3 else a_ref.at[c]
        return remote(src, ag.at[x - 1, c], a_s.at[x, c], a_r.at[x, c], {"col": across if x == 2 else mate})

    def m_copy(x):
        src = amg.at[1] if x == 3 else am_ref
        return remote(src, amg.at[x - 1], m_s.at[x], m_r.at[x], {"col": across if x == 2 else mate})

    for j in range(1, R):
        q_copy(j, row).start()
    m_copy(2).start()
    m_copy(1).start()
    for i in range(panels_held):
        for j in range(1, R):
            p_copy(j, i, row).start()
    for c in range(C):
        a_copy(2, c).start()
    for c in range(C):
        a_copy(1, c).start()

    lane_high = (lax.broadcasted_iota(jnp.int32, (1, 128), 1) >= 64).astype(jnp.float32)
    zero = jnp.zeros((4, 16, 128), jnp.bfloat16)

    def spread(tiles, keys, m):
        value = zero
        for tile, key in zip(tiles, keys):
            value = jnp.where((key == jnp.bfloat16(2 * m))[None], tile, value)
        return value.reshape(64, 128)

    def expand_panel(vals, meta, i, q):
        for w in range(width_p):
            tiles, keys = [], []
            for half in range(2):
                tile = vals[i, w, :, half * 128 : half * 128 + 128]
                tiles += [tile.reshape(4, 16, 128), swap_halves(tile).reshape(4, 16, 128)]
                keys += masks_of(meta[i, 2 * w + half : 2 * w + half + 1, :], lane_high)
            for m in range(CB // 2):
                dense[q, w * 64 : w * 64 + 64, m * 128 : m * 128 + 128] = spread(tiles, keys, m)

    def expand_chunk(x, c):
        vals = a_ref if x == 0 else ag.at[x - 1]
        meta = am_ref if x == 0 else amg.at[x - 1]
        for k in range(held):
            for b in range(blocks):
                tile = vals[c, b, k]
                tiles = [tile.reshape(4, 16, 128), swap_halves(tile).reshape(4, 16, 128)]
                line = b * held + k
                keys = masks_of(meta[c, line : line + 1, :], lane_high)
                for m in range(CB // 2):
                    lhs[x * held + k, c, b * 64 : b * 64 + 64, m * 128 : m * 128 + 128] = spread(tiles, keys, m)

    def product(c, q):
        term = jnp.dot(lhs[slot_ref[q], c], dense[q], preferred_element_type=jnp.float32)
        return term.reshape(part.shape[1:])

    def add(c, q):
        part[c] += product(c, q)

    def take_panel(n):
        j, i = 1 + n // panels_held, n % panels_held
        slot = lax.rem(row + R - j, R)
        if i == 0:
            q_copy(j, slot).wait_recv()
        p_copy(j, i, slot).wait_recv()
        expand_panel(pg.at[slot], pqg.at[slot], i, slot * panels_held + i)
        return slot * panels_held + i

    @pl.loop(0, panels_held)
    def _(i):
        expand_panel(p_ref, pq_ref, i, row * panels_held + i)

    @pl.loop(0, C)
    def _(c):
        part[c] = jnp.zeros(part.shape[1:], jnp.float32)
        expand_chunk(0, c)

    m_copy(1).wait_recv()
    m_copy(2).wait_recv()
    m_copy(3).start()
    others = (R - 1) * panels_held
    each = -(-(others - 1) // (C - 1))
    taken = []
    for c in range(C):
        a_copy(2, c).wait_recv()
        a_copy(3, c).start()
        a_copy(1, c).wait_recv()
        expand_chunk(1, c)
        expand_chunk(2, c)
        if c == 0:
            m_copy(3).wait_recv()
        a_copy(3, c).wait_recv()
        expand_chunk(3, c)

        @pl.loop(0, panels_held)
        def _(i):
            add(c, row * panels_held + i)

        for q in taken:
            add(c, q)
        if c:
            for n in range((c - 1) * each, min(c * each, others - 1)):
                q = take_panel(n)
                taken.append(q)

                @pl.loop(0, c + 1)
                def _(earlier):
                    add(earlier, q)

    last = take_panel(others - 1)

    wide_out = part.shape[3]

    def u_copies(d, c):
        to = {"layer": layer + 1}
        return (
            remote(txs.at[c, d], up_sc.at[c, d], us_s.at[c, d], us_r.at[c, d], to),
            remote(tx.at[c, d], up_in.at[c, d], u_s.at[c, d], u_r.at[c, d], to),
        )

    def d_copies(d, c):
        to = {"layer": layer - 1}
        return (
            remote(txs.at[c, d], down_sc.at[c, d], ds_s.at[c, d], ds_r.at[c, d], to),
            remote(tx.at[c, d], down_in.at[c, d], d_s.at[c, d], d_r.at[c, d], to),
        )

    def send(copies, d, c, value):
        high, low, scale = encode(value)
        tx[c, d, :, :wide_out] = high
        tx[c, d, :, wide_out:] = low
        txs[c, d] = scale
        for copy in copies(d, c):
            copy.start()

    def received(copies, ref, scales, d, c):
        for copy in copies(d, c):
            copy.wait_recv()
        return decode(ref[c, d, :, :wide_out], ref[c, d, :, wide_out:], scales[c, d])

    @pl.loop(0, C)
    def _(c):
        add(c, last)

        @pl.when(layer == 0)
        def _():
            for d in range(L - 1, 0, -1):
                send(u_copies, d, c, part[c, d])

        @pl.when(layer == L - 1)
        def _():
            for d in range(L - 1):
                send(d_copies, d, c, part[c, d])

    def forward_up(c, d):
        @pl.when((layer > 0) & (layer < d))
        def _():
            send(u_copies, d, c, part[c, d] + received(u_copies, up_in, up_sc, d, c))

    def forward_down(c, d):
        @pl.when((layer < L - 1) & (layer > d))
        def _():
            send(d_copies, d, c, part[c, d] + received(d_copies, down_in, down_sc, d, c))

    def o_copy(c, slot):
        return remote(fin.at[c], got.at[slot], o_s.at[c], o_r.at[slot], {"col": c})

    @pl.loop(0, C)
    def _(c):
        for k in range(L - 1):
            @pl.when(layer >= L // 2)
            def _():
                forward_down(c, k)

            forward_up(c, L - 1 - k)

            @pl.when(layer < L // 2)
            def _():
                forward_down(c, k)

        @pl.when(layer > 0)
        def _():
            part[c, layer] += received(u_copies, up_in, up_sc, layer, c)

        @pl.when(layer < L - 1)
        def _():
            part[c, layer] += received(d_copies, down_in, down_sc, layer, c)

        result = part[c, layer].astype(jnp.bfloat16)

        @pl.when(col == c)
        def _():
            got[c] = result

        @pl.when(col != c)
        def _():
            fin[c] = result
            o_copy(c, col).start()

    for c in range(C):
        @pl.when(col != c)
        def _():
            o_copy(c, c).wait_recv()

        out_ref[:, c * CB * 64 : (c + 1) * CB * 64] = got[c]

    for j in range(1, R):
        q_copy(j, row).wait_send()
        for i in range(panels_held):
            p_copy(j, i, row).wait_send()
    for x in range(1, 4):
        m_copy(x).wait_send()
        for c in range(C):
            a_copy(x, c).wait_send()
    for c in range(C):
        for d in range(L):
            @pl.when(layer < d)
            def _():
                for copy in u_copies(d, c):
                    copy.wait_send()

            @pl.when(layer > d)
            def _():
                for copy in d_copies(d, c):
                    copy.wait_send()

        @pl.when(col != c)
        def _():
            o_copy(c, c).wait_send()


def lanes_of(cols, count):
    slots = cols.shape[-1]
    valid = jnp.arange(slots) < count[..., None]
    key = jnp.where(valid, cols, -64).astype(jnp.float32)
    wide = jnp.broadcast_to(key[..., None], key.shape + (64,))
    return wide.reshape(cols.shape[:-1] + (slots // 2, 128))


def body(sizes, a_vals, a_cols, a_count, panel_map, p_vals, p_cols, p_count):
    R, C, L = sizes
    rows_blk, _, held, side, wide = a_vals.shape
    blocks = rows_blk // C
    panels_held, width_p = p_vals.shape[1], p_vals.shape[2]
    a = a_vals.reshape(C, blocks, held, side, wide)
    lines = blocks * held
    am = lanes_of(a_cols[:, 0], a_count[:, 0]).reshape(C, lines, 128)
    pad = -lines % 8
    am = jnp.pad(am, ((0, 0), (0, pad), (0, 0)))
    p = p_vals.reshape(panels_held, width_p, side, p_vals.shape[-1])
    pq = lanes_of(p_cols[0, :, :, 0], p_count[0, :, :, 0]).reshape(panels_held, 2 * width_p, 128)
    col = lax.axis_index("col")
    layer_map = lax.dynamic_index_in_dim(panel_map, lax.axis_index("layer"), 0, keepdims=False)
    sections = jnp.arange(layer_map.shape[0], dtype=jnp.int32)
    owner = sections // held
    mate = col + 1 - 2 * (col % 2)
    across = (col + 2) % 4
    place = jnp.where(owner == col, 0, jnp.where(owner == mate, 1, jnp.where(owner == across, 2, 3)))
    place = (place * held + sections % held).astype(jnp.int32)
    slots = jnp.sum(jnp.where(layer_map[None, :] == sections[:, None], place[None, :], 0), axis=1)
    piece = blocks * side // L
    width = CB * side
    f32, bf16 = jnp.float32, jnp.bfloat16
    sems = pltpu.SemaphoreType.DMA
    coded = pltpu.VMEM((C, L, piece, width + width // 2), jnp.int16)
    scales = pltpu.VMEM((C, L, 8, 128), f32)
    vmem = pl.BlockSpec(memory_space=pltpu.VMEM)
    return pl.pallas_call(
        functools.partial(kernel, sizes),
        out_shape=jax.ShapeDtypeStruct((piece, C * width), bf16),
        in_specs=[pl.BlockSpec(memory_space=pltpu.SMEM), vmem, vmem, vmem, vmem],
        out_specs=vmem,
        scratch_shapes=[
            pltpu.VMEM((3,) + a.shape, bf16),
            pltpu.VMEM((3,) + am.shape, f32),
            pltpu.VMEM((R,) + p.shape, bf16),
            pltpu.VMEM((R,) + pq.shape, f32),
            pltpu.VMEM((R * panels_held, width_p * side, width), bf16),
            pltpu.VMEM((C * held, C, blocks * side, width_p * side), bf16),
            pltpu.VMEM((C, L, piece, width), f32),
            *[coded, scales] * 3,
            pltpu.VMEM((C, piece, width), bf16),
            pltpu.VMEM((C, piece, width), bf16),
            sems((R, panels_held)), sems((R, panels_held)), sems((R,)), sems((R,)),
            sems((4, C)), sems((4, C)), sems((4,)), sems((4,)),
            *[sems((C, L))] * 8,
            sems((C,)), sems((C,)),
        ],
        compiler_params=pltpu.CompilerParams(
            collective_id=0, has_side_effects=True, vmem_limit_bytes=56 * 1024 * 1024
        ),
        cost_estimate=pl.CostEstimate(flops=7 * 10**9, bytes_accessed=3 * 10**6, transcendentals=0),
    )(slots, a, am, p, pq)


def solution(mesh):
    placed = (
        P("row", "layer", "col", None, None),
        P("row", "layer", "col", None),
        P("row", "layer", "col"),
        P(),
        P("layer", "row", None, "col", None, None),
        P("layer", "row", None, "col", None),
        P("layer", "row", None, "col"),
    )
    sizes = (mesh.shape["row"], mesh.shape["col"], mesh.shape["layer"])
    return jax.shard_map(
        functools.partial(body, sizes),
        mesh=mesh,
        in_specs=placed,
        out_specs=P(("row", "col", "layer"), None),
        check_vma=False,
    )
```

```python
import functools

import jax
import jax.numpy as jnp
from jax import lax
from jax.experimental import pallas as pl
from jax.experimental.pallas import tpu as pltpu
from jax.sharding import PartitionSpec as P

CB = 8
MESH = pl.DeviceIdType.MESH


def swap_halves(tile):
    return pltpu.roll(tile.astype(jnp.float32), 64, 1).astype(jnp.bfloat16)


def masks_of(meta_row, lane_high):
    straight = (meta_row - lane_high).astype(jnp.float32)
    swapped = pltpu.roll(meta_row, 64, 1) - lane_high
    wide = lambda row: jnp.broadcast_to(row, (16, 128)).astype(jnp.bfloat16)
    return wide(straight), wide(swapped)


FULL = float(2**22)


def encode(value):
    rows, width = value.shape
    grouped = value.reshape(rows // 8, 8, width)
    most = jnp.max(jnp.abs(grouped), axis=0)
    most = functools.reduce(jnp.maximum, [most[:, i : i + 128] for i in range(0, width, 128)])
    most = jnp.maximum(most, 1e-31)
    factor = jnp.concatenate([FULL / most] * (width // 128), axis=1)
    fixed = jnp.round(grouped * factor[None]).astype(jnp.int32).reshape(rows, width)
    high = lax.shift_right_arithmetic(fixed, 8).astype(jnp.int16)
    low = fixed & 255
    low = (low[:, : width // 2] * 256 + low[:, width // 2 :] - 32768).astype(jnp.int16)
    return high, low, most * (1.0 / FULL)


def decode(high, low, scale):
    rows, width = high.shape
    pair = low.astype(jnp.int32) + 32768
    low = jnp.concatenate([lax.shift_right_arithmetic(pair, 8), pair & 255], axis=1)
    fixed = (high.astype(jnp.int32) * 256 + low).astype(jnp.float32)
    factor = jnp.concatenate([scale] * (width // 128), axis=1)
    return (fixed.reshape(rows // 8, 8, width) * factor[None]).reshape(rows, width)


def kernel(
    sizes,
    slot_ref, a_ref, am_ref, p_ref, pq_ref, out_ref,
    ag, amg, pg, pqg, dense, lhs, part, tx, txs, up_in, up_sc, down_in, down_sc, fin, got,
    p_s, p_r, q_s, q_r, a_s, a_r, m_s, m_r, u_s, u_r, us_s, us_r, d_s, d_r, ds_s, ds_r, o_s, o_r,
):
    R, C, L = sizes
    row, col, layer = lax.axis_index("row"), lax.axis_index("col"), lax.axis_index("layer")
    panels_held, width_p = p_ref.shape[0], p_ref.shape[1]
    blocks, held = a_ref.shape[1], a_ref.shape[2]
    mate = col + 1 - 2 * lax.rem(col, 2)
    across = lax.rem(col + 2, 4)

    barrier = pltpu.get_barrier_semaphore()
    for j in range(1, R):
        pl.semaphore_signal(barrier, inc=1, device_id={"row": lax.rem(row + j, R)}, device_id_type=MESH)
    for j in range(1, C):
        pl.semaphore_signal(barrier, inc=1, device_id={"col": lax.rem(col + j, C)}, device_id_type=MESH)

    @pl.when(layer > 0)
    def _():
        pl.semaphore_signal(barrier, inc=1, device_id={"layer": layer - 1}, device_id_type=MESH)

    @pl.when(layer < L - 1)
    def _():
        pl.semaphore_signal(barrier, inc=1, device_id={"layer": layer + 1}, device_id_type=MESH)

    ends = (layer > 0).astype(jnp.int32) + (layer < L - 1).astype(jnp.int32)
    pl.semaphore_wait(barrier, R - 1 + C - 1 + ends)

    def remote(src, dst, send, recv, device):
        return pltpu.make_async_remote_copy(
            src_ref=src, dst_ref=dst, send_sem=send, recv_sem=recv, device_id=device, device_id_type=MESH
        )

    def p_copy(j, i, slot):
        return remote(p_ref.at[i], pg.at[slot, i], p_s.at[j, i], p_r.at[j, i], {"row": lax.rem(row + j, R)})

    def q_copy(j, slot):
        return remote(pq_ref, pqg.at[slot], q_s.at[j], q_r.at[j], {"row": lax.rem(row + j, R)})

    def a_copy(x, c):
        src = ag.at[1, c] if x == 3 else a_ref.at[c]
        return remote(src, ag.at[x - 1, c], a_s.at[x, c], a_r.at[x, c], {"col": across if x == 2 else mate})

    def m_copy(x):
        src = amg.at[1] if x == 3 else am_ref
        return remote(src, amg.at[x - 1], m_s.at[x], m_r.at[x], {"col": across if x == 2 else mate})

    for j in range(1, R):
        q_copy(j, row).start()
    m_copy(2).start()
    m_copy(1).start()
    others = (R - 1) * panels_held

    def p_nth(n):
        return p_copy(1 + n // panels_held, n % panels_held, row)

    for n in range(min(2, others)):
        p_nth(n).start()
    for c in range(2):
        a_copy(2, c).start()
    for c in range(C):
        a_copy(1, c).start()

    def next_p(n):
        if n + 2 < others:
            p_nth(n).wait_send()
            p_nth(n + 2).start()

    lane_high = (lax.broadcasted_iota(jnp.int32, (1, 128), 1) >= 64).astype(jnp.float32)
    zero = jnp.zeros((4, 16, 128), jnp.bfloat16)

    def spread(tiles, keys, m):
        value = zero
        for tile, key in zip(tiles, keys):
            value = jnp.where((key == jnp.bfloat16(2 * m))[None], tile, value)
        return value.reshape(64, 128)

    def expand_panel(vals, meta, i, q):
        for w in range(width_p):
            tiles, keys = [], []
            for half in range(2):
                tile = vals[i, w, :, half * 128 : half * 128 + 128]
                tiles += [tile.reshape(4, 16, 128), swap_halves(tile).reshape(4, 16, 128)]
                keys += masks_of(meta[i, 2 * w + half : 2 * w + half + 1, :], lane_high)
            for m in range(CB // 2):
                dense[q, w * 64 : w * 64 + 64, m * 128 : m * 128 + 128] = spread(tiles, keys, m)

    def expand_chunk(x, c):
        vals = a_ref if x == 0 else ag.at[x - 1]
        meta = am_ref if x == 0 else amg.at[x - 1]
        for k in range(held):
            for b in range(blocks):
                tile = vals[c, b, k]
                tiles = [tile.reshape(4, 16, 128), swap_halves(tile).reshape(4, 16, 128)]
                line = b * held + k
                keys = masks_of(meta[c, line : line + 1, :], lane_high)
                for m in range(CB // 2):
                    lhs[x * held + k, c, b * 64 : b * 64 + 64, m * 128 : m * 128 + 128] = spread(tiles, keys, m)

    def product(c, q):
        term = jnp.dot(lhs[slot_ref[q], c], dense[q], preferred_element_type=jnp.float32)
        return term.reshape(part.shape[1:])

    def add(c, q):
        part[c] += product(c, q)

    def take_panel(n):
        j, i = 1 + n // panels_held, n % panels_held
        slot = lax.rem(row + R - j, R)
        if i == 0:
            q_copy(j, slot).wait_recv()
        p_copy(j, i, slot).wait_recv()
        expand_panel(pg.at[slot], pqg.at[slot], i, slot * panels_held + i)
        return slot * panels_held + i

    @pl.loop(0, panels_held)
    def _(i):
        expand_panel(p_ref, pq_ref, i, row * panels_held + i)

    @pl.loop(0, C)
    def _(c):
        part[c] = jnp.zeros(part.shape[1:], jnp.float32)
        expand_chunk(0, c)

    m_copy(1).wait_recv()
    m_copy(2).wait_recv()
    m_copy(3).start()
    each = -(-(others - 1) // (C - 1))
    taken = []
    for c in range(C):
        a_copy(2, c).wait_recv()
        a_copy(3, c).start()
        if c + 2 < C:
            a_copy(2, c).wait_send()
            a_copy(2, c + 2).start()
        for n in range(c, others) if c == C - 1 else (c,):
            next_p(n)
        a_copy(1, c).wait_recv()
        expand_chunk(1, c)
        expand_chunk(2, c)
        if c == 0:
            m_copy(3).wait_recv()
        a_copy(3, c).wait_recv()
        expand_chunk(3, c)

        @pl.loop(0, panels_held)
        def _(i):
            add(c, row * panels_held + i)

        for q in taken:
            add(c, q)
        if c:
            for n in range((c - 1) * each, min(c * each, others - 1)):
                q = take_panel(n)
                taken.append(q)

                @pl.loop(0, c + 1)
                def _(earlier):
                    add(earlier, q)

    last = take_panel(others - 1)

    wide_out = part.shape[3]

    def u_copies(d, c):
        to = {"layer": layer + 1}
        return (
            remote(txs.at[c, d], up_sc.at[c, d], us_s.at[c, d], us_r.at[c, d], to),
            remote(tx.at[c, d], up_in.at[c, d], u_s.at[c, d], u_r.at[c, d], to),
        )

    def d_copies(d, c):
        to = {"layer": layer - 1}
        return (
            remote(txs.at[c, d], down_sc.at[c, d], ds_s.at[c, d], ds_r.at[c, d], to),
            remote(tx.at[c, d], down_in.at[c, d], d_s.at[c, d], d_r.at[c, d], to),
        )

    def stage(d, c, value):
        high, low, scale = encode(value)
        tx[c, d, :, :wide_out] = high
        tx[c, d, :, wide_out:] = low
        txs[c, d] = scale

    def send(copies, d, c, value):
        stage(d, c, value)
        launch(copies, d, c)

    def launch(copies, d, c):
        for copy in copies(d, c):
            copy.start()

    def received(copies, ref, scales, d, c):
        for copy in copies(d, c):
            copy.wait_recv()
        return decode(ref[c, d, :, :wide_out], ref[c, d, :, wide_out:], scales[c, d])

    def send_all(copies, order, c):
        order = list(order)
        for n, d in enumerate(order):
            stage(d, c, part[c, d])
            if n >= 2:
                sent(copies, order[n - 2], c)
            else:
                @pl.when(c > 0)
                def _():
                    sent(copies, order[len(order) - 2 + n], c - 1)
            launch(copies, d, c)

    def sent(copies, d, c):
        for copy in copies(d, c):
            copy.wait_send()

    @pl.loop(0, C)
    def _(c):
        add(c, last)

        @pl.when(layer == 0)
        def _():
            send_all(u_copies, range(L - 1, 0, -1), c)

        @pl.when(layer == L - 1)
        def _():
            send_all(d_copies, range(L - 1), c)

    def forward_up(c, d):
        @pl.when((layer > 0) & (layer < d))
        def _():
            send(u_copies, d, c, part[c, d] + received(u_copies, up_in, up_sc, d, c))

    def forward_down(c, d):
        @pl.when((layer < L - 1) & (layer > d))
        def _():
            send(d_copies, d, c, part[c, d] + received(d_copies, down_in, down_sc, d, c))

    def o_copy(c, slot):
        return remote(fin.at[c], got.at[slot], o_s.at[c], o_r.at[slot], {"col": c})

    @pl.loop(0, C)
    def _(c):
        for k in range(L - 1):
            @pl.when(layer >= L // 2)
            def _():
                forward_down(c, k)

            forward_up(c, L - 1 - k)

            @pl.when(layer < L // 2)
            def _():
                forward_down(c, k)

        @pl.when(layer > 0)
        def _():
            part[c, layer] += received(u_copies, up_in, up_sc, layer, c)

        @pl.when(layer < L - 1)
        def _():
            part[c, layer] += received(d_copies, down_in, down_sc, layer, c)

        result = part[c, layer].astype(jnp.bfloat16)

        @pl.when(col == c)
        def _():
            got[c] = result

        @pl.when(col != c)
        def _():
            fin[c] = result
            o_copy(c, col).start()

    for c in range(C):
        @pl.when(col != c)
        def _():
            o_copy(c, c).wait_recv()

        out_ref[:, c * CB * 64 : (c + 1) * CB * 64] = got[c]

    for j in range(1, R):
        q_copy(j, row).wait_send()
    for n in range(max(others - 2, 0), others):
        p_nth(n).wait_send()
    for x in range(1, 4):
        m_copy(x).wait_send()
        for c in range(C - 2 if x == 2 else 0, C):
            a_copy(x, c).wait_send()
    for c in range(C):
        for d in range(L):
            @pl.when((layer < d) & ((layer > 0) | ((c == C - 1) & (d <= 2))))
            def _():
                sent(u_copies, d, c)

            @pl.when((layer > d) & ((layer < L - 1) | ((c == C - 1) & (d >= L - 3))))
            def _():
                sent(d_copies, d, c)

        @pl.when(col != c)
        def _():
            o_copy(c, c).wait_send()


def lanes_of(cols, count):
    slots = cols.shape[-1]
    valid = jnp.arange(slots) < count[..., None]
    key = jnp.where(valid, cols, -64).astype(jnp.float32)
    wide = jnp.broadcast_to(key[..., None], key.shape + (64,))
    return wide.reshape(cols.shape[:-1] + (slots // 2, 128))


def body(sizes, a_vals, a_cols, a_count, panel_map, p_vals, p_cols, p_count):
    R, C, L = sizes
    rows_blk, _, held, side, wide = a_vals.shape
    blocks = rows_blk // C
    panels_held, width_p = p_vals.shape[1], p_vals.shape[2]
    a = a_vals.reshape(C, blocks, held, side, wide)
    lines = blocks * held
    am = lanes_of(a_cols[:, 0], a_count[:, 0]).reshape(C, lines, 128)
    pad = -lines % 8
    am = jnp.pad(am, ((0, 0), (0, pad), (0, 0)))
    p = p_vals.reshape(panels_held, width_p, side, p_vals.shape[-1])
    pq = lanes_of(p_cols[0, :, :, 0], p_count[0, :, :, 0]).reshape(panels_held, 2 * width_p, 128)
    col = lax.axis_index("col")
    layer_map = lax.dynamic_index_in_dim(panel_map, lax.axis_index("layer"), 0, keepdims=False)
    sections = jnp.arange(layer_map.shape[0], dtype=jnp.int32)
    owner = sections // held
    mate = col + 1 - 2 * (col % 2)
    across = (col + 2) % 4
    place = jnp.where(owner == col, 0, jnp.where(owner == mate, 1, jnp.where(owner == across, 2, 3)))
    place = (place * held + sections % held).astype(jnp.int32)
    slots = jnp.sum(jnp.where(layer_map[None, :] == sections[:, None], place[None, :], 0), axis=1)
    piece = blocks * side // L
    width = CB * side
    f32, bf16 = jnp.float32, jnp.bfloat16
    sems = pltpu.SemaphoreType.DMA
    coded = pltpu.VMEM((C, L, piece, width + width // 2), jnp.int16)
    scales = pltpu.VMEM((C, L, 8, 128), f32)
    vmem = pl.BlockSpec(memory_space=pltpu.VMEM)
    return pl.pallas_call(
        functools.partial(kernel, sizes),
        out_shape=jax.ShapeDtypeStruct((piece, C * width), bf16),
        in_specs=[pl.BlockSpec(memory_space=pltpu.SMEM), vmem, vmem, vmem, vmem],
        out_specs=vmem,
        scratch_shapes=[
            pltpu.VMEM((3,) + a.shape, bf16),
            pltpu.VMEM((3,) + am.shape, f32),
            pltpu.VMEM((R,) + p.shape, bf16),
            pltpu.VMEM((R,) + pq.shape, f32),
            pltpu.VMEM((R * panels_held, width_p * side, width), bf16),
            pltpu.VMEM((C * held, C, blocks * side, width_p * side), bf16),
            pltpu.VMEM((C, L, piece, width), f32),
            *[coded, scales] * 3,
            pltpu.VMEM((C, piece, width), bf16),
            pltpu.VMEM((C, piece, width), bf16),
            sems((R, panels_held)), sems((R, panels_held)), sems((R,)), sems((R,)),
            sems((4, C)), sems((4, C)), sems((4,)), sems((4,)),
            *[sems((C, L))] * 8,
            sems((C,)), sems((C,)),
        ],
        compiler_params=pltpu.CompilerParams(
            collective_id=0, has_side_effects=True, vmem_limit_bytes=56 * 1024 * 1024
        ),
        cost_estimate=pl.CostEstimate(flops=7 * 10**9, bytes_accessed=3 * 10**6, transcendentals=0),
    )(slots, a, am, p, pq)


def solution(mesh):
    placed = (
        P("row", "layer", "col", None, None),
        P("row", "layer", "col", None),
        P("row", "layer", "col"),
        P(),
        P("layer", "row", None, "col", None, None),
        P("layer", "row", None, "col", None),
        P("layer", "row", None, "col"),
    )
    sizes = (mesh.shape["row"], mesh.shape["col"], mesh.shape["layer"])
    return jax.shard_map(
        functools.partial(body, sizes),
        mesh=mesh,
        in_specs=placed,
        out_specs=P(("row", "col", "layer"), None),
        check_vma=False,
    )
```
